512 devices in a mesh: samp: 32 (over z, x_lo), par: 16 (over y, x_hi, core).
Axes of the slice: x: 4 (x_hi: 2, x_lo: 2; x = x_hi * 2 + x_lo), y: 4, z: 16, core: 2. Of those that a mesh axis runs over, the one named last changes fastest.
Arguments:
- logder: bfloat16 [16384, 16384], P('samp', 'par'), may hold values from -6 to 6
- block_of: int32 [16384], P('samp'), may hold values from 0 to 31, as said below
- plan: int32 [2, 32], replicated, may hold values from 0 to 31, as said below
Outputs:
- tiles: float32 [3, 16384, 512], P(None, ('samp', 'par'))
The draws below stay inside these ranges and needn't reach their ends.
Inputs may be any that keep to these rules, and one draw needn't show every extreme that they name: `block_of`: among the 512 samples of each index of samp, every block is named exactly 16 times. Each row pairs the blocks: plan[r, plan[r, b]] = b and plan[r, b] != b; the two rounds share no pair (rounds of a round-robin tournament).
All inputs are finite; a program needn't handle non-finite values.
Results may differ from the reference program's by a relative error of at most 0.0003.
Values may be sent and summed in bfloat16 or wider, within the bound.
A program may use at most 64 MiB of HBM per device.

```python
import math
import jax
import jax.numpy as jnp
from jax import lax

PC = 16384
B = 512
ROUNDS = 2
NS = 16384
N_SAMP = 32


def draw_block_of(key, part):
    key = jax.random.fold_in(key, 1)
    keys = jax.random.split(key, N_SAMP)
    base = jnp.tile(jnp.arange(N_SAMP, dtype=jnp.int32), B // N_SAMP)
    rows = jax.vmap(lambda k: jax.random.permutation(k, base))(keys)
    return rows.reshape(-1).astype(jnp.int32)


def draw_plan(key, part):
    key = jax.random.fold_in(key, 2)
    key_perm, key_first, key_step = jax.random.split(key, 3)
    relabel = jax.random.permutation(key_perm, N_SAMP).astype(jnp.int32)
    modulus = N_SAMP - 1
    first = jax.random.randint(key_first, (), 0, modulus)
    second = (first + jax.random.randint(key_step, (), 1, modulus)) % modulus
    player = jnp.arange(N_SAMP, dtype=jnp.int32)

    def one_round(turn):
        circle = jnp.where(player == modulus, turn, jnp.where(player == turn, modulus, (2 * turn - player) % modulus))
        return jnp.zeros((N_SAMP,), jnp.int32).at[relabel].set(relabel[circle])
    return jnp.stack([one_round(first), one_round(second)]).astype(jnp.int32)


def block_scale(rng, extent, shards, low, high):
    def one(axis_at, parts):
        draws = jax.random.uniform(jax.random.fold_in(jax.random.fold_in(rng, 6), axis_at), (parts,), jnp.float32, low / len(shards), high / len(shards))
        return jnp.repeat(jnp.exp(draws), extent[axis_at] // parts).reshape((-1,) + (1,) * (len(extent) - axis_at - 1))

    gain = one(*shards[0])
    for cut in shards[1:]:
        gain = gain * one(*cut)
    return gain


def normal_values(own_key, extent, scale, most, pieces=(), kind=jnp.bfloat16):
    entries = jax.random.normal(own_key, extent, jnp.float32) * scale
    if len(pieces) > 0:
        entries = block_scale(own_key, extent, pieces, -0.22, 0.18) * entries
    return jnp.clip(entries, min=-most, max=most).astype(kind)


def setup_inputs(seed: int = 0) -> dict:
    streams_of = jax.random.split(jax.random.key(seed), 4)
    logder = normal_values(streams_of[0], (NS, PC), 1.0, 6.0, ((0, 32), (1, 16)))
    block_of = draw_block_of(jax.random.fold_in(streams_of[3], 71), 0)
    plan = draw_plan(jax.random.fold_in(streams_of[3], 71), 0)
    return dict(logder=logder, block_of=block_of, plan=plan)


def reference(logder, block_of, plan):
    order = jnp.argsort(block_of, stable=True).astype(jnp.int32).reshape(N_SAMP, B)
    scale = 1.0 / math.sqrt(PC)
    own = jnp.arange(N_SAMP, dtype=jnp.int32)
    partner = jnp.concatenate([own[None, :], plan.astype(jnp.int32)], axis=0)
    firsts = jnp.tile(own, ROUNDS + 1)

    def single(pair):
        first_rows = logder[order[pair[0]]]
        other_rows = logder[order[pair[1]]]
        prod = lax.dot_general(first_rows, other_rows, (((1,), (1,)), ((), ())), preferred_element_type=jnp.float32)
        return prod * scale
    result = lax.map(single, (firsts, partner.reshape(-1)))
    return result.reshape(ROUNDS + 1, N_SAMP * B, B)
```

```python
import functools
import math

import jax
import jax.numpy as jnp
from jax import lax
from jax.experimental import pallas as pl
from jax.experimental.pallas import tpu as pltpu
from jax.sharding import PartitionSpec as P

MESH = pl.DeviceIdType.MESH
NS = 32
NZ = 16
CHIPS = 8
CHIP_OFFSETS = ((0, 1), (1, 0), (3, 0), (1, 1), (3, 1), (2, 0), (2, 1))


def layout_kernel(plan, block_of, place, table, seen):
    def clear(b, carry):
        seen[b] = 0
        return carry

    lax.fori_loop(0, NS, clear, 0)

    def cycle(first, base):
        def walk():
            def more(state):
                return (state[0] != first) & (state[1] < NZ)

            def step(state):
                return plan[1, plan[0, state[0]]], state[1] + 1

            _, m = lax.while_loop(more, step, (plan[1, plan[0, first]], jnp.int32(1)))

            def put(b, k, after, before):
                seen[b] = 1
                out = k < m
                t = jnp.where(out, 2 * (base + k), 2 * (base + 2 * m - 1 - k) + 1)
                nxt = jnp.where(out, jnp.where(k == m - 1, 2, 0), jnp.where(k == 2 * m - 1, 2, 1))
                prv = jnp.where(out, jnp.where(k == 0, 2, 1), jnp.where(k == m, 2, 0))
                table[0, b] = t
                table[after, t] = nxt
                table[before, t] = prv

            def pair(i, u):
                v = plan[0, u]
                put(u, 2 * i, 1, 2)
                put(v, 2 * i + 1, 2, 1)
                return plan[1, v]

            lax.fori_loop(0, m, pair, first)
            return base + m

        return lax.cond(seen[first] == 0, walk, lambda: base)

    lax.fori_loop(0, NS, cycle, jnp.int32(0))

    rows = block_of.shape[1]
    block_at = lax.broadcasted_iota(jnp.int32, (NS, rows), 0)
    mine = block_at == block_of[...]
    earlier = lax.broadcasted_iota(jnp.int32, (rows, rows), 0) < lax.broadcasted_iota(jnp.int32, (rows, rows), 1)
    rank = jnp.dot(mine.astype(jnp.bfloat16), earlier.astype(jnp.bfloat16), preferred_element_type=jnp.float32)
    start = jnp.zeros((NS, rows), jnp.int32)
    for b in range(NS):
        start = jnp.where(block_at == b, table[0, b] * (rows // NS), start)
    spot = jnp.where(mine, rank.astype(jnp.int32) + start, 0)
    place[...] = jnp.sum(spot, axis=0, keepdims=True)


def main_kernel(
    scale,
    table,
    place,
    logder,
    out,
    sorted_rows,
    own,
    near,
    own_part,
    own_pair,
    own_share,
    own_in,
    edge_part,
    edge_pair,
    edge_share,
    edge_in,
    own_piece,
    own_mid,
    own_turn,
    own_home,
    edge_piece,
    edge_mid,
    edge_turn,
    edge_home,
    send,
    rows_recv,
    near_recv,
    pair_recv,
    own_chip_recv,
    edge_chip_recv,
    mid_recv,
    home_recv,
):
    me = lax.axis_index("samp")
    par = lax.axis_index("par")
    z, x = me // 2, me % 2
    chip, core = par // 2, par % 2
    y, x_hi = chip // 2, chip % 2
    rows = logder.shape[0]
    per = rows // NS
    share = rows // (2 * CHIPS)

    def ring(k):
        return jnp.where(k % 2 == 1, (k + 1) // 2, NS - k // 2)

    def to_samp(s):
        return {"samp": s}

    def chip_at(offset):
        return lax.rem(y + offset[0], 4) * 2 + lax.rem(x_hi + offset[1], 2)

    def remote(src, dst, send_sem, recv_sem, device):
        return pltpu.make_async_remote_copy(
            src_ref=src, dst_ref=dst, send_sem=send_sem, recv_sem=recv_sem, device_id=device, device_id_type=MESH
        )

    def await_bytes(ref, sem):
        pltpu.make_async_copy(ref, ref, sem).wait()

    barrier = pltpu.get_barrier_semaphore()

    def greet(k, carry):
        pl.semaphore_signal(barrier, inc=1, device_id=to_samp(lax.rem(me + k, NS)), device_id_type=MESH)
        return carry

    lax.fori_loop(1, NS, greet, 0)
    pl.semaphore_signal(barrier, inc=1, device_id={"par": chip * 2 + 1 - core}, device_id_type=MESH)
    for offset in CHIP_OFFSETS:
        pl.semaphore_signal(barrier, inc=1, device_id={"par": chip_at(offset) * 2 + core}, device_id_type=MESH)

    pick = (lax.broadcasted_iota(jnp.int32, (rows, rows), 0) == place[...]).astype(jnp.bfloat16)
    sorted_rows[...] = jnp.dot(pick, logder[...], preferred_element_type=jnp.float32).astype(jnp.bfloat16)
    pl.semaphore_wait(barrier, NS - 1 + 1 + len(CHIP_OFFSETS))

    def chunk(s):
        return pl.ds(pl.multiple_of(s * per, per), per)

    def send_rows(k, carry):
        to = lax.rem(me + ring(k), NS)
        remote(sorted_rows.at[chunk(to)], own.at[chunk(me)], send.at[0], rows_recv.at[k], to_samp(to)).start()
        return carry

    lax.fori_loop(1, NS, send_rows, 0)
    own[chunk(me), :] = sorted_rows[chunk(me), :]

    above = lax.rem(z + 1, NZ) * 2 + x
    below = lax.rem(z + NZ - 1, NZ) * 2 + x
    across = z * 2 + 1 - x

    def pass_on(s):
        for slot, to in ((1, above), (0, below), (2, across)):
            remote(own.at[chunk(s)], near.at[slot, chunk(s)], send.at[1], near_recv.at[slot], to_samp(to)).start()

    pass_on(me)

    def arrive(k, carry):
        s = lax.rem(me + NS - ring(k), NS)
        await_bytes(own.at[chunk(s)], rows_recv.at[k])
        pass_on(s)
        return carry

    lax.fori_loop(1, NS, arrive, 0)

    def tile_of(other):
        return lax.dot_general(own[...], other, (((1,), (1,)), ((), ())), preferred_element_type=jnp.float32)

    def to_pair(part, pair, n):
        copy = remote(part.at[1 - core], pair, send.at[2 + n], pair_recv.at[n], {"par": chip * 2 + 1 - core})
        copy.start()
        return copy

    def to_chips(held, landing, sem, n):
        copies = []
        for i, offset in enumerate(CHIP_OFFSETS):
            to = chip_at(offset)
            copy = remote(held.at[to], landing.at[i], send.at[4 + n], sem.at[i], {"par": to * 2 + core})
            copy.start()
            copies.append(copy)
        return copies

    def exchange(piece, landing, sem, n):
        def one(k, carry):
            to = lax.rem(me + ring(k), NS)
            remote(piece.at[to], landing.at[me], send.at[n], sem, to_samp(to)).start()
            return carry

        lax.fori_loop(1, NS, one, 0)
        landing[me] = piece[me]

    def await_exchange(landing, sem):
        await_bytes(landing.at[pl.ds(0, NS - 1)], sem)

    def turn(mid, turned):
        for b in range(NS):
            turned[b] = mid[table[0, b]]

    product = tile_of(own[...])
    for c in range(2):
        for j in range(CHIPS):
            at = (2 * j + c) * share
            own_part[c, j] = product[at : at + share]
    to_pair(own_part, own_pair, 0).wait_recv()
    own_share[...] = own_part[core] + own_pair[...]
    copies = to_chips(own_share, own_in, own_chip_recv, 0)
    total = own_share[chip]
    for i, copy in enumerate(copies):
        copy.wait_recv()
        total += own_in[i]
    total *= scale
    for i in range(NS):
        a, l = (i // 4) * (share // 8), (i % 4) * 128
        own_piece[i] = total[a : a + share // 8, l : l + 128]
    exchange(own_piece, own_mid, mid_recv.at[0], 6)

    for slot in range(3):
        await_bytes(near.at[slot], near_recv.at[slot])
    for r in range(2):
        product = tile_of(near[table[1 + r, me]])
        for c in range(2):
            for j in range(CHIPS):
                at = (2 * j + c) * share
                edge_part[c, j, r] = product[at : at + share]
    to_pair(edge_part, edge_pair, 1).wait_recv()
    edge_share[...] = edge_part[core] + edge_pair[...]
    copies = to_chips(edge_share, edge_in, edge_chip_recv, 1)

    await_exchange(own_mid, mid_recv.at[0])
    turn(own_mid, own_turn)
    exchange(own_turn, own_home, home_recv.at[0], 7)

    total = edge_share[chip]
    for i, copy in enumerate(copies):
        copy.wait_recv()
        total += edge_in[i]
    total *= scale
    for i in range(NS):
        a, l = ((i % 16) // 4) * (share // 4), (i % 4) * 128
        edge_piece[i] = total[i // 16, a : a + share // 4, l : l + 128]
    exchange(edge_piece, edge_mid, mid_recv.at[1], 8)

    await_exchange(own_home, home_recv.at[0])
    for i in range(NS):
        a, l = (i // 4) * (share // 8), (i % 4) * 128
        out[0, a : a + share // 8, l : l + 128] = own_home[i]

    await_exchange(edge_mid, mid_recv.at[1])
    turn(edge_mid, edge_turn)
    exchange(edge_turn, edge_home, home_recv.at[1], 9)
    await_exchange(edge_home, home_recv.at[1])
    for i in range(NS):
        a, l = ((i % 16) // 4) * (share // 4), (i % 4) * 128
        out[1 + i // 16, a : a + share // 4, l : l + 128] = edge_home[i]

    await_bytes(own.at[pl.ds(0, rows - per)], send.at[0])
    await_bytes(near, send.at[1])
    await_bytes(own_pair, send.at[2])
    await_bytes(edge_pair, send.at[3])
    await_bytes(own_in, send.at[4])
    await_bytes(edge_in, send.at[5])
    for n, piece in ((6, own_piece), (7, own_turn), (8, edge_piece), (9, edge_turn)):
        await_exchange(piece, send.at[n])


def shards(logder, block_of, plan):
    rows, columns = logder.shape
    share = rows // (2 * CHIPS)
    smem = pl.BlockSpec(memory_space=pltpu.SMEM)
    vmem = pl.BlockSpec(memory_space=pltpu.VMEM)
    place, table = pl.pallas_call(
        layout_kernel,
        name="layout",
        out_shape=(jax.ShapeDtypeStruct((1, rows), jnp.int32), jax.ShapeDtypeStruct((3, NS), jnp.int32)),
        in_specs=[smem, vmem],
        out_specs=(vmem, smem),
        scratch_shapes=[pltpu.SMEM((NS,), jnp.int32)],
    )(plan, block_of.reshape(1, rows))
    scale = 1.0 / math.sqrt(columns * lax.axis_size("par"))
    f32, bf16 = jnp.float32, jnp.bfloat16
    own_pieces = pltpu.VMEM((NS, share // 8, 128), f32)
    edge_pieces = pltpu.VMEM((NS, share // 4, 128), f32)
    return pl.pallas_call(
        functools.partial(main_kernel, scale),
        name="tiles",
        out_shape=jax.ShapeDtypeStruct((3, share, rows), f32),
        in_specs=[smem, vmem, vmem],
        out_specs=vmem,
        scratch_shapes=[
            pltpu.VMEM((rows, columns), bf16),
            pltpu.VMEM((rows, columns), bf16),
            pltpu.VMEM((3, rows, columns), bf16),
            pltpu.VMEM((2, CHIPS, share, rows), f32),
            pltpu.VMEM((CHIPS, share, rows), f32),
            pltpu.VMEM((CHIPS, share, rows), f32),
            pltpu.VMEM((CHIPS - 1, share, rows), f32),
            pltpu.VMEM((2, CHIPS, 2, share, rows), f32),
            pltpu.VMEM((CHIPS, 2, share, rows), f32),
            pltpu.VMEM((CHIPS, 2, share, rows), f32),
            pltpu.VMEM((CHIPS - 1, 2, share, rows), f32),
            own_pieces,
            own_pieces,
            own_pieces,
            own_pieces,
            edge_pieces,
            edge_pieces,
            edge_pieces,
            edge_pieces,
            pltpu.SemaphoreType.DMA((10,)),
            pltpu.SemaphoreType.DMA((NS,)),
            pltpu.SemaphoreType.DMA((3,)),
            pltpu.SemaphoreType.DMA((2,)),
            pltpu.SemaphoreType.DMA((CHIPS - 1,)),
            pltpu.SemaphoreType.DMA((CHIPS - 1,)),
            pltpu.SemaphoreType.DMA((2,)),
            pltpu.SemaphoreType.DMA((2,)),
        ],
        compiler_params=pltpu.CompilerParams(
            collective_id=0, has_side_effects=True, vmem_limit_bytes=48 * 1024 * 1024
        ),
    )(table, place, logder)


def solution(mesh):
    return jax.shard_map(
        shards,
        mesh=mesh,
        in_specs=(P("samp", "par"), P("samp"), P()),
        out_specs=P(None, ("samp", "par"), None),
        check_vma=False,
    )
```

```python
import functools
import math

import jax
import jax.numpy as jnp
from jax import lax
from jax.experimental import pallas as pl
from jax.experimental.pallas import tpu as pltpu
from jax.sharding import PartitionSpec as P

MESH = pl.DeviceIdType.MESH
NS = 32
NZ = 16
CHIPS = 8
NY = 4
GROUPS = ((0, 256), (256, 128), (384, 128))
STEPS = 16
WINDOW = 5
BITS = (-0x55555556, -0x33333334, -0x0F0F0F10, -0x00FF0100, -0x00010000)


def ladder(plan):
    block = first = k = seen = jnp.int32(0)
    walk = []
    for j in range(NS):
        seen = seen | lax.shift_left(jnp.int32(1), block)
        after = plan[j % 2, block]
        closed = None
        if j % 2 == 1:
            closed = after == first
        walk.append((block, k, closed))
        if closed is None:
            block, k = after, k + 1
        else:
            free = ~seen & (seen + 1)
            lowest = jnp.int32(0)
            for i, bits in enumerate(BITS):
                lowest = lowest + jnp.where((free & bits) != 0, 1 << i, 0)
            first = jnp.where(closed, lowest, first)
            block = jnp.where(closed, lowest, after)
            k = jnp.where(closed, 0, k + 1)
    steps = []
    length = jnp.int32(0)
    for j in reversed(range(NS)):
        block, k, closed = walk[j]
        if closed is not None:
            length = jnp.where(closed, k + 1, length)
        m = lax.shift_right_logical(length, 1)
        out = k < m
        position = jnp.where(out, j + k, j - 3 * k + 2 * length - 1)
        onward = jnp.where(out, jnp.where(k == m - 1, 2, 0), jnp.where(k == length - 1, 2, 1))
        back = jnp.where(out, jnp.where(k == 0, 2, 1), jnp.where(k == m, 2, 0))
        steps.append((block, position, (onward, back) if j % 2 == 0 else (back, onward)))
    return steps


def tiles_kernel(scale, logder, block_of, plan, out, *scratch):
    (
        raw, blocks, pairs, place, table, sorted_rows, own, near, parts, pair_in, shares, y_in, halves, x_in,
        piece, mid, turned, home, local, send, rows_send, rows_recv, near_send, near_recv, pair_recv, y_recv, x_recv, mid_recv, home_recv,
    ) = scratch
    me = lax.axis_index("samp")
    par = lax.axis_index("par")
    z, x = me // 2, me % 2
    chip, core = par // 2, par % 2
    y, x_hi = chip // 2, chip % 2
    rows = raw.shape[0]
    per = rows // NS
    share = rows // (2 * CHIPS)
    units = len(parts)

    def ring(k):
        return jnp.where(k % 2 == 1, (k + 1) // 2, NS - k // 2)

    def along_y(d):
        return {"par": (lax.rem(y + d, NY) * 2 + x_hi) * 2 + core}

    other_core = {"par": chip * 2 + 1 - core}
    other_x = {"par": (y * 2 + 1 - x_hi) * 2 + core}

    def remote(src, dst, send_sem, recv_sem, device):
        return pltpu.make_async_remote_copy(
            src_ref=src, dst_ref=dst, send_sem=send_sem, recv_sem=recv_sem, device_id=device, device_id_type=MESH
        )

    def await_bytes(ref, sem):
        pltpu.make_async_copy(ref, ref, sem).wait()

    arrivals = [
        pltpu.make_async_copy(plan, pairs, local.at[0]),
        pltpu.make_async_copy(block_of, blocks, local.at[1]),
        pltpu.make_async_copy(logder, raw, local.at[2]),
    ]
    for copy in arrivals:
        copy.start()

    barrier = pltpu.get_barrier_semaphore()

    def greet(k, carry):
        pl.semaphore_signal(barrier, inc=1, device_id={"samp": lax.rem(me + k, NS)}, device_id_type=MESH)
        return carry

    lax.fori_loop(1, NS, greet, 0)
    in_plane = [other_core, other_x] + [along_y(d) for d in range(1, NY)]
    for device in in_plane:
        pl.semaphore_signal(barrier, inc=1, device_id=device, device_id_type=MESH)

    arrivals[0].wait()
    steps = ladder(pairs)
    arrivals[1].wait()
    block_at = lax.broadcasted_iota(jnp.int32, (NS, rows), 0)
    mine = block_at == blocks[...]
    earlier = lax.broadcasted_iota(jnp.int32, (rows, rows), 0) < lax.broadcasted_iota(jnp.int32, (rows, rows), 1)
    rank = jnp.dot(mine.astype(jnp.bfloat16), earlier.astype(jnp.bfloat16), preferred_element_type=jnp.float32)
    lane = lax.broadcasted_iota(jnp.int32, place.shape, 1)
    start = jnp.zeros((NS, rows), jnp.int32)
    placed = jnp.zeros(place.shape, jnp.int32)
    sides = [jnp.int32(0), jnp.int32(0)]
    for block, position, where in steps:
        start = jnp.where(block_at == block, position * per, start)
        placed = jnp.where(lane == block, position, placed)
        for r in range(2):
            sides[r] = jnp.where(position == me, where[r], sides[r])
    place[...] = placed
    to_table = pltpu.make_async_copy(place, table, local.at[3])
    to_table.start()
    spot = jnp.where(mine, rank.astype(jnp.int32) + start, 0)
    spot = jnp.sum(spot, axis=0, keepdims=True)
    pick = (lax.broadcasted_iota(jnp.int32, (rows, rows), 0) == spot).astype(jnp.bfloat16)
    arrivals[2].wait()
    sorted_rows[...] = jnp.dot(pick, raw[...], preferred_element_type=jnp.float32).astype(jnp.bfloat16)
    pl.semaphore_wait(barrier, NS - 1 + len(in_plane))

    def chunk(s):
        return pl.ds(pl.multiple_of(s * per, per), per)

    def send_rows(k, carry):
        to = lax.rem(me + ring(NS - k), NS)
        remote(sorted_rows.at[chunk(to)], own.at[chunk(me)], rows_send, rows_recv.at[NS - k], {"samp": to}).start()
        return carry

    lax.fori_loop(1, NS, send_rows, 0)
    own[chunk(me), :] = sorted_rows[chunk(me), :]
    to_table.wait()

    def arrive(k, carry):
        s = lax.rem(me + NS - ring(k), NS)
        await_bytes(own.at[chunk(s)], rows_recv.at[k])
        return carry

    lax.fori_loop(1, NS, arrive, 0)

    above = lax.rem(z + 1, NZ) * 2 + x
    below = lax.rem(z + NZ - 1, NZ) * 2 + x
    across = z * 2 + 1 - x
    step_rows = rows // STEPS
    handed = [0]

    def hand_on(upto):
        for i in range(handed[0], upto):
            if i >= WINDOW:
                await_bytes(near[0].at[:, pl.ds(0, step_rows)], near_send.at[i - WINDOW])
            part = pl.ds(i * step_rows, step_rows)
            g = sum(i * step_rows >= first for first, _ in GROUPS) - 1
            there = pl.ds(i * step_rows - GROUPS[g][0], step_rows)
            for slot, to in ((1, above), (0, below), (2, across)):
                landing = near[g].at[slot, there]
                remote(own.at[part], landing, near_send.at[i], near_recv.at[g, slot], {"samp": to}).start()
        handed[0] = max(handed[0], upto)

    def multiply(other):
        return lax.dot_general(own[...], other, (((1,), (1,)), ((), ())), preferred_element_type=jnp.float32)

    def to_pair(u):
        remote(parts[u].at[1 - core], pair_in[u], send.at[u], pair_recv.at[u], other_core).start()

    def to_ys(u):
        await_bytes(pair_in[u], pair_recv.at[u])
        shares[u][...] = parts[u][core] + pair_in[u][...]
        for d in (1, 3, 2):
            to = pl.ds(2 * lax.rem(y + d, NY), 2)
            remote(shares[u].at[to], y_in[u].at[d - 1], send.at[units + u], y_recv.at[u, d - 1], along_y(d)).start()

    def to_x(u):
        total = shares[u][pl.ds(2 * y, 2)]
        for i in range(NY - 1):
            await_bytes(y_in[u].at[i], y_recv.at[u, i])
            total += y_in[u][i]
        halves[u][...] = total
        remote(halves[u].at[1 - x_hi], x_in[u], send.at[2 * units + u], x_recv.at[u], other_x).start()

    def whole(u):
        await_bytes(x_in[u], x_recv.at[u])
        return (halves[u][x_hi] + x_in[u][...]) * scale

    def own_tile(u):
        product = multiply(own[...])
        for c in range(2):
            for j in range(CHIPS):
                at = (2 * j + c) * share
                parts[u][c, j] = product[at : at + share]
        to_pair(u)

    def partner_tiles(u, g):
        for slot in range(3):
            await_bytes(near[g].at[slot], near_recv.at[g, slot])
        for r in range(2):
            product = multiply(near[g][sides[r]])
            for c in range(2):
                for j in range(CHIPS):
                    at = (2 * j + c) * share
                    parts[u][c, j, r] = product[at : at + share]
        to_pair(u)

    def exchange(src, landing, sem, recv_sem):
        def one(k, carry):
            to = lax.rem(me + ring(NS - k), NS)
            remote(src.at[to], landing.at[me], sem, recv_sem, {"samp": to}).start()
            return carry

        lax.fori_loop(1, NS, one, 0)
        landing[me] = src[me]

    def await_exchange(ref, sem):
        await_bytes(ref.at[pl.ds(0, NS - 1)], sem)

    sent_mid, sent_home = 3 * units, 3 * units + 2

    def to_mid(n):
        exchange(piece[n], mid[n], send.at[sent_mid + n], mid_recv.at[n])

    def to_home(n):
        await_exchange(mid[n], mid_recv.at[n])
        for b in range(NS):
            turned[n][b] = mid[n][table[0, b]]
        exchange(turned[n], home[n], send.at[sent_home + n], home_recv.at[n])

    def own_pieces():
        total = whole(0)
        for i in range(16):
            a, l = 8 * (i // 4), 128 * (i % 4)
            piece[0][i] = total[a : a + 8, l : l + 128]

    def first_pieces():
        total = whole(1)
        for i in range(16):
            r, a, l = i // 8, 8 * (i % 8 // 2), 128 * (i % 2)
            piece[0][16 + i] = total[r, a : a + 8, l : l + 128]

    def later_pieces(h):
        total = whole(2 + h)
        for i in range(16):
            r, a = i // 8, 4 * (i % 8)
            piece[1][16 * h + i] = total[r, a : a + 4]

    hand_on(WINDOW)
    own_tile(0)
    hand_on(WINDOW + 2)
    to_ys(0)
    hand_on(12)
    to_x(0)
    hand_on(13)
    partner_tiles(1, 0)
    hand_on(14)
    to_ys(1)
    hand_on(STEPS)
    own_pieces()
    partner_tiles(2, 1)
    to_ys(2)
    to_x(1)
    partner_tiles(3, 2)
    to_x(2)
    to_ys(3)
    first_pieces()
    to_mid(0)
    later_pieces(0)
    to_x(3)
    later_pieces(1)
    to_mid(1)
    to_home(0)
    to_home(1)
    await_exchange(home[0], home_recv.at[0])
    for i in range(16):
        a, l = 8 * (i // 4), 128 * (i % 4)
        out[0, a : a + 8, l : l + 128] = home[0][i]
        r, a, l = i // 8, 8 * (i % 8 // 2), 128 * (i % 2)
        out[1 + r, a : a + 8, l : l + 128] = home[0][16 + i]
    await_exchange(home[1], home_recv.at[1])
    for i in range(NS):
        h, r, a = i // 16, i % 16 // 8, 4 * (i % 8)
        out[1 + r, a : a + 4, 256 + 128 * h : 384 + 128 * h] = home[1][i]

    await_bytes(own.at[pl.ds(0, rows - per)], rows_send)
    for i in range(STEPS - WINDOW, STEPS):
        await_bytes(near[0].at[:, pl.ds(0, step_rows)], near_send.at[i])
    for u in range(units):
        await_bytes(pair_in[u], send.at[u])
        await_bytes(y_in[u], send.at[units + u])
        await_bytes(x_in[u], send.at[2 * units + u])
    for n in range(2):
        await_exchange(piece[n], send.at[sent_mid + n])
        await_exchange(turned[n], send.at[sent_home + n])


def shards(logder, block_of, plan):
    rows, columns = logder.shape
    share = rows // (2 * CHIPS)
    anywhere = pl.BlockSpec(memory_space=pl.ANY)
    scale = 1.0 / math.sqrt(columns * lax.axis_size("par"))
    f32, bf16, i32 = jnp.float32, jnp.bfloat16, jnp.int32
    kinds = ((share, rows),) + tuple((2, share, count) for _, count in GROUPS)
    sizes = (8, 4)

    def buffers(*lead):
        return [pltpu.VMEM(lead + kind, f32) for kind in kinds]

    def pieces():
        return [pltpu.VMEM((NS, size, 128), f32) for size in sizes]

    sems = pltpu.SemaphoreType.DMA
    units = len(kinds)
    return pl.pallas_call(
        functools.partial(tiles_kernel, scale),
        name="tiles",
        out_shape=jax.ShapeDtypeStruct((3, share, rows), f32),
        in_specs=[anywhere, anywhere, anywhere],
        out_specs=pl.BlockSpec(memory_space=pltpu.VMEM),
        scratch_shapes=[
            pltpu.VMEM((rows, columns), bf16),
            pltpu.VMEM((1, rows), i32),
            pltpu.SMEM((2, NS), i32),
            pltpu.VMEM((8, 128), i32),
            pltpu.SMEM((8, 128), i32),
            pltpu.VMEM((rows, columns), bf16),
            pltpu.VMEM((rows, columns), bf16),
            [pltpu.VMEM((3, count, columns), bf16) for _, count in GROUPS],
            buffers(2, CHIPS),
            buffers(CHIPS),
            buffers(CHIPS),
            buffers(NY - 1, 2),
            buffers(2),
            buffers(),
            pieces(),
            pieces(),
            pieces(),
            pieces(),
            sems((4,)),
            sems((3 * units + 2 * len(sizes),)),
            sems,
            sems((NS,)),
            sems((STEPS,)),
            sems((len(GROUPS), 3)),
            sems((units,)),
            sems((units, NY - 1)),
            sems((units,)),
            sems((len(sizes),)),
            sems((len(sizes),)),
        ],
        compiler_params=pltpu.CompilerParams(
            collective_id=0, has_side_effects=True, vmem_limit_bytes=62 * 1024 * 1024
        ),
    )(logder, block_of.reshape(1, rows), plan)


def solution(mesh):
    return jax.shard_map(
        shards,
        mesh=mesh,
        in_specs=(P("samp", "par"), P("samp"), P()),
        out_specs=P(None, ("samp", "par"), None),
        check_vma=False,
    )
```

```python
import functools
import math

import jax
import jax.numpy as jnp
from jax import lax
from jax.experimental import pallas as pl
from jax.experimental.pallas import tpu as pltpu
from jax.sharding import PartitionSpec as P

MESH = pl.DeviceIdType.MESH
NS = 32
NZ = 16
CHIPS = 8
NY = 4
CHIP_OFFSETS = ((2, 1), (1, 1), (3, 1), (0, 1), (2, 0), (1, 0), (3, 0))
GROUPS = ((0, 256), (256, 128), (384, 128))
STEPS = 16
WINDOW = 8
DIRECT = (3,)
EARLY = 2
BITS = (-0x55555556, -0x33333334, -0x0F0F0F10, -0x00FF0100, -0x00010000)


def ladder(plan):
    block = first = k = seen = jnp.int32(0)
    walk = []
    for j in range(NS):
        seen = seen | lax.shift_left(jnp.int32(1), block)
        after = plan[j % 2, block]
        closed = None
        if j % 2 == 1:
            closed = after == first
        walk.append((block, k, closed))
        if closed is None:
            block, k = after, k + 1
        else:
            free = ~seen & (seen + 1)
            lowest = jnp.int32(0)
            for i, bits in enumerate(BITS):
                lowest = lowest + jnp.where((free & bits) != 0, 1 << i, 0)
            first = jnp.where(closed, lowest, first)
            block = jnp.where(closed, lowest, after)
            k = jnp.where(closed, 0, k + 1)
    steps = []
    length = jnp.int32(0)
    for j in reversed(range(NS)):
        block, k, closed = walk[j]
        if closed is not None:
            length = jnp.where(closed, k + 1, length)
        m = lax.shift_right_logical(length, 1)
        out = k < m
        position = jnp.where(out, j + k, j - 3 * k + 2 * length - 1)
        onward = jnp.where(out, jnp.where(k == m - 1, 2, 0), jnp.where(k == length - 1, 2, 1))
        back = jnp.where(out, jnp.where(k == 0, 2, 1), jnp.where(k == m, 2, 0))
        steps.append((block, position, (onward, back) if j % 2 == 0 else (back, onward)))
    return steps


def tiles_kernel(scale, logder, block_of, plan, out, *scratch):
    (
        raw, blocks, pairs, place, table, sorted_rows, own, near, parts, pair_in, shares, y_in, halves, x_in,
        piece, mid, turned, home, local, send, rows_send, rows_recv, near_send, near_recv, pair_recv, y_recv, x_recv, chip_recv, mid_recv, home_recv,
    ) = scratch
    me = lax.axis_index("samp")
    par = lax.axis_index("par")
    z, x = me // 2, me % 2
    chip, core = par // 2, par % 2
    y, x_hi = chip // 2, chip % 2
    rows = raw.shape[0]
    per = rows // NS
    share = rows // (2 * CHIPS)
    units = len(parts)

    def ring(k):
        return jnp.where(k % 2 == 1, (k + 1) // 2, NS - k // 2)

    def along_y(d):
        return {"par": (lax.rem(y + d, NY) * 2 + x_hi) * 2 + core}

    def chip_at(offset):
        return lax.rem(y + offset[0], NY) * 2 + lax.rem(x_hi + offset[1], 2)

    def at_chip(to):
        return {"par": to * 2 + core}

    other_core = {"par": chip * 2 + 1 - core}
    other_x = {"par": (y * 2 + 1 - x_hi) * 2 + core}

    def remote(src, dst, send_sem, recv_sem, device):
        return pltpu.make_async_remote_copy(
            src_ref=src, dst_ref=dst, send_sem=send_sem, recv_sem=recv_sem, device_id=device, device_id_type=MESH
        )

    def await_bytes(ref, sem):
        pltpu.make_async_copy(ref, ref, sem).wait()

    arrivals = [
        pltpu.make_async_copy(plan, pairs, local.at[0]),
        pltpu.make_async_copy(block_of, blocks, local.at[1]),
        pltpu.make_async_copy(logder, raw, local.at[2]),
    ]
    for copy in arrivals:
        copy.start()

    barrier = pltpu.get_barrier_semaphore()

    def greet(k, carry):
        pl.semaphore_signal(barrier, inc=1, device_id={"samp": lax.rem(me + k, NS)}, device_id_type=MESH)
        return carry

    lax.fori_loop(1, NS, greet, 0)
    in_plane = [other_core] + [at_chip(chip_at(offset)) for offset in CHIP_OFFSETS]
    for device in in_plane:
        pl.semaphore_signal(barrier, inc=1, device_id=device, device_id_type=MESH)

    arrivals[0].wait()
    steps = ladder(pairs)
    arrivals[1].wait()
    block_at = lax.broadcasted_iota(jnp.int32, (NS, rows), 0)
    mine = block_at == blocks[...]
    earlier = lax.broadcasted_iota(jnp.int32, (rows, rows), 0) < lax.broadcasted_iota(jnp.int32, (rows, rows), 1)
    rank = jnp.dot(mine.astype(jnp.bfloat16), earlier.astype(jnp.bfloat16), preferred_element_type=jnp.float32)
    lane = lax.broadcasted_iota(jnp.int32, place.shape, 1)
    start = jnp.zeros((NS, rows), jnp.int32)
    placed = jnp.zeros(place.shape, jnp.int32)
    sides = [jnp.int32(0), jnp.int32(0)]
    for block, position, where in steps:
        start = jnp.where(block_at == block, position * per, start)
        placed = jnp.where(lane == block, position, placed)
        for r in range(2):
            sides[r] = jnp.where(position == me, where[r], sides[r])
    place[...] = placed
    to_table = pltpu.make_async_copy(place, table, local.at[3])
    to_table.start()
    spot = jnp.where(mine, rank.astype(jnp.int32) + start, 0)
    spot = jnp.sum(spot, axis=0, keepdims=True)
    pick = (lax.broadcasted_iota(jnp.int32, (rows, rows), 0) == spot).astype(jnp.bfloat16)
    arrivals[2].wait()
    sorted_rows[...] = jnp.dot(pick, raw[...], preferred_element_type=jnp.float32).astype(jnp.bfloat16)
    pl.semaphore_wait(barrier, NS - 1 + len(in_plane))

    def chunk(s):
        return pl.ds(pl.multiple_of(s * per, per), per)

    def send_rows(k, carry):
        to = lax.rem(me + ring(NS - k), NS)
        remote(sorted_rows.at[chunk(to)], own.at[chunk(me)], rows_send, rows_recv.at[NS - k], {"samp": to}).start()
        return carry

    lax.fori_loop(1, NS, send_rows, 0)
    own[chunk(me), :] = sorted_rows[chunk(me), :]
    to_table.wait()

    above = lax.rem(z + 1, NZ) * 2 + x
    below = lax.rem(z + NZ - 1, NZ) * 2 + x
    across = z * 2 + 1 - x
    def hand_on_chunk(s):
        for slot, to in ((1, above), (0, below), (2, across)):
            landing = near[0].at[slot, chunk(s)]
            remote(own.at[chunk(s)], landing, near_send.at[s // 2], near_recv.at[0, slot], {"samp": to}).start()

    @pl.when(me < 2 * EARLY)
    def _():
        hand_on_chunk(me)

    def arrive(k, carry):
        s = lax.rem(me + NS - ring(k), NS)
        await_bytes(own.at[chunk(s)], rows_recv.at[k])

        @pl.when(s < 2 * EARLY)
        def _():
            hand_on_chunk(s)

        return carry

    lax.fori_loop(1, NS, arrive, 0)

    step_rows = rows // STEPS
    handed = [EARLY]

    def hand_on(upto):
        for i in range(handed[0], upto):
            if i >= WINDOW:
                await_bytes(near[0].at[:, pl.ds(0, step_rows)], near_send.at[i - WINDOW])
            part = pl.ds(i * step_rows, step_rows)
            g = sum(i * step_rows >= first for first, _ in GROUPS) - 1
            there = pl.ds(i * step_rows - GROUPS[g][0], step_rows)
            for slot, to in ((1, above), (0, below), (2, across)):
                landing = near[g].at[slot, there]
                remote(own.at[part], landing, near_send.at[i], near_recv.at[g, slot], {"samp": to}).start()
        handed[0] = max(handed[0], upto)

    def multiply(other):
        return lax.dot_general(own[...], other, (((1,), (1,)), ((), ())), preferred_element_type=jnp.float32)

    def to_pair(u):
        remote(parts[u].at[1 - core], pair_in[u], send.at[u], pair_recv.at[u], other_core).start()

    def to_ys(u):
        await_bytes(pair_in[u], pair_recv.at[u])
        shares[u][...] = parts[u][core] + pair_in[u][...]
        if u in DIRECT:
            for i, offset in enumerate(CHIP_OFFSETS):
                to = chip_at(offset)
                remote(shares[u].at[to], y_in[u].at[i], send.at[units + u], chip_recv.at[u, i], at_chip(to)).start()
            return
        for d in (2, 1, 3):
            to = pl.ds(2 * lax.rem(y + d, NY), 2)
            remote(shares[u].at[to], y_in[u].at[d - 1], send.at[units + u], y_recv.at[u, d - 1], along_y(d)).start()

    def to_x(u):
        if u in DIRECT:
            return
        total = shares[u][pl.ds(2 * y, 2)]
        for i in range(NY - 1):
            await_bytes(y_in[u].at[i], y_recv.at[u, i])
            total += y_in[u][i]
        halves[u][...] = total
        remote(halves[u].at[1 - x_hi], x_in[u], send.at[2 * units + u], x_recv.at[u], other_x).start()

    def to_x(u):
        if u in DIRECT:
            return
        total = shares[u][pl.ds(2 * y, 2)]
        for i in range(NY - 1):
            await_bytes(y_in[u].at[i], y_recv.at[u, i])
            total += y_in[u][i]
        halves[u][...] = total
        remote(halves[u].at[1 - x_hi], x_in[u], send.at[2 * units + u], x_recv.at[u], other_x).start()

    def to_chips(u):
        await_bytes(pair_in[u], pair_recv.at[u])
        shares[u][...] = parts[u][core] + pair_in[u][...]
        for i, offset in enumerate(CHIP_OFFSETS):
            to = chip_at(offset)
            remote(shares[u].at[to], y_in[u].at[i], send.at[units + u], chip_recv.at[u, i], at_chip(to)).start()

    def whole(u):
        if u in DIRECT:
            total = shares[u][chip]
            for i in range(len(CHIP_OFFSETS)):
                await_bytes(y_in[u].at[i], chip_recv.at[u, i])
                total += y_in[u][i]
            return total * scale
        await_bytes(x_in[u], x_recv.at[u])
        return (halves[u][x_hi] + x_in[u][...]) * scale

    def own_tile(u):
        product = multiply(own[...])
        for c in range(2):
            for j in range(CHIPS):
                at = (2 * j + c) * share
                parts[u][c, j] = product[at : at + share]
        to_pair(u)

    def partner_tiles(u, g):
        for slot in range(3):
            await_bytes(near[g].at[slot], near_recv.at[g, slot])
        for r in range(2):
            product = multiply(near[g][sides[r]])
            for c in range(2):
                for j in range(CHIPS):
                    at = (2 * j + c) * share
                    parts[u][c, j, r] = product[at : at + share]
        to_pair(u)

    def exchange(src, landing, sem, recv_sem):
        def one(k, carry):
            to = lax.rem(me + ring(NS - k), NS)
            remote(src.at[to], landing.at[me], sem, recv_sem, {"samp": to}).start()
            return carry

        lax.fori_loop(1, NS, one, 0)
        landing[me] = src[me]

    def await_exchange(ref, sem):
        await_bytes(ref.at[pl.ds(0, NS - 1)], sem)

    sent_mid, sent_home = 3 * units, 3 * units + 3

    def to_mid(n):
        exchange(piece[n], mid[n], send.at[sent_mid + n], mid_recv.at[n])

    def to_home(n):
        await_exchange(mid[n], mid_recv.at[n])
        for b in range(NS):
            turned[n][b] = mid[n][table[0, b]]
        exchange(turned[n], home[n], send.at[sent_home + n], home_recv.at[n])

    def own_pieces():
        total = whole(0)
        for i in range(NS):
            a, l = 4 * (i // 4), 128 * (i % 4)
            piece[0][i] = total[a : a + 4, l : l + 128]

    def first_pieces():
        total = whole(1)
        for i in range(NS):
            r, a, l = i // 16, 4 * (i % 16 // 2), 128 * (i % 2)
            piece[1][i] = total[r, a : a + 4, l : l + 128]

    def later_pieces(h, total):
        for i in range(16):
            r, a = i // 8, 4 * (i % 8)
            piece[2][16 * h + i] = total[r, a : a + 4]

    hand_on(WINDOW)
    own_tile(0)
    hand_on(WINDOW + 2)
    to_ys(0)
    hand_on(12)
    to_x(0)
    hand_on(13)
    partner_tiles(1, 0)
    hand_on(14)
    to_ys(1)
    hand_on(STEPS)
    own_pieces()
    to_mid(0)
    partner_tiles(2, 1)
    to_ys(2)
    partner_tiles(3, 2)
    to_x(1)
    to_ys(3)
    to_x(2)
    to_home(0)
    first_pieces()
    to_mid(1)
    later_pieces(0, whole(2))
    later_pieces(1, whole(3))
    to_mid(2)
    await_exchange(home[0], home_recv.at[0])
    for i in range(NS):
        a, l = 4 * (i // 4), 128 * (i % 4)
        out[0, a : a + 4, l : l + 128] = home[0][i]
    to_home(1)
    to_home(2)
    await_exchange(home[1], home_recv.at[1])
    for i in range(NS):
        r, a, l = i // 16, 4 * (i % 16 // 2), 128 * (i % 2)
        out[1 + r, a : a + 4, l : l + 128] = home[1][i]
    await_exchange(home[2], home_recv.at[2])
    for i in range(NS):
        h, r, a = i // 16, i % 16 // 8, 4 * (i % 8)
        out[1 + r, a : a + 4, 256 + 128 * h : 384 + 128 * h] = home[2][i]

    await_bytes(own.at[pl.ds(0, rows - per)], rows_send)
    for i in range(STEPS - WINDOW, STEPS):
        await_bytes(near[0].at[:, pl.ds(0, step_rows)], near_send.at[i])
    for u in range(units):
        await_bytes(pair_in[u], send.at[u])
        await_bytes(y_in[u], send.at[units + u])
        if u not in DIRECT:
            await_bytes(x_in[u], send.at[2 * units + u])
    for n in range(3):
        await_exchange(piece[n], send.at[sent_mid + n])
        await_exchange(turned[n], send.at[sent_home + n])


def shards(logder, block_of, plan):
    rows, columns = logder.shape
    share = rows // (2 * CHIPS)
    hbm = pl.BlockSpec(memory_space=pltpu.HBM)
    scale = 1.0 / math.sqrt(columns * lax.axis_size("par"))
    f32, bf16, i32 = jnp.float32, jnp.bfloat16, jnp.int32
    kinds = ((share, rows),) + tuple((2, share, count) for _, count in GROUPS)
    sizes = (4, 4, 4)

    def buffers(*lead):
        return [pltpu.VMEM(lead + kind, f32) for kind in kinds]

    def pieces():
        return [pltpu.VMEM((NS, size, 128), f32) for size in sizes]

    sems = pltpu.SemaphoreType.DMA
    units = len(kinds)
    return pl.pallas_call(
        functools.partial(tiles_kernel, scale),
        name="tiles",
        out_shape=jax.ShapeDtypeStruct((3, share, rows), f32),
        in_specs=[hbm, hbm, hbm],
        out_specs=pl.BlockSpec(memory_space=pltpu.VMEM),
        scratch_shapes=[
            pltpu.VMEM((rows, columns), bf16),
            pltpu.VMEM((1, rows), i32),
            pltpu.SMEM((2, NS), i32),
            pltpu.VMEM((8, 128), i32),
            pltpu.SMEM((8, 128), i32),
            pltpu.VMEM((rows, columns), bf16),
            pltpu.VMEM((rows, columns), bf16),
            [pltpu.VMEM((3, count, columns), bf16) for _, count in GROUPS],
            buffers(2, CHIPS),
            buffers(CHIPS),
            buffers(CHIPS),
            [pltpu.VMEM(((CHIPS - 1,) if u in DIRECT else (NY - 1, 2)) + kind, f32) for u, kind in enumerate(kinds)],
            buffers(2),
            buffers(),
            pieces(),
            pieces(),
            pieces(),
            pieces(),
            sems((4,)),
            sems((3 * units + 2 * len(sizes),)),
            sems,
            sems((NS,)),
            sems((STEPS,)),
            sems((len(GROUPS), 3)),
            sems((units,)),
            sems((units, NY - 1)),
            sems((units,)),
            sems((units, CHIPS - 1)),
            sems((len(sizes),)),
            sems((len(sizes),)),
        ],
        compiler_params=pltpu.CompilerParams(
            collective_id=0, has_side_effects=True, vmem_limit_bytes=62 * 1024 * 1024
        ),
    )(logder, block_of.reshape(1, rows), plan)


def solution(mesh):
    return jax.shard_map(
        shards,
        mesh=mesh,
        in_specs=(P("samp", "par"), P("samp"), P()),
        out_specs=P(None, ("samp", "par"), None),
        check_vma=False,
    )
```

```python
import functools
import math

import jax
import jax.numpy as jnp
from jax import lax
from jax.experimental import pallas as pl
from jax.experimental.pallas import tpu as pltpu
from jax.sharding import PartitionSpec as P

MESH = pl.DeviceIdType.MESH
NS = 32
NZ = 16
CHIPS = 8
NY = 4
CHIP_OFFSETS = ((2, 1), (1, 1), (3, 1), (0, 1), (2, 0), (1, 0), (3, 0))
GROUPS = ((0, 256), (256, 128), (384, 128))
STEPS = 16
WINDOW = 8
DIRECT = (3,)
EARLY = 4
BITS = (-0x55555556, -0x33333334, -0x0F0F0F10, -0x00FF0100, -0x00010000)


def ladder(plan):
    block = first = k = seen = jnp.int32(0)
    walk = []
    for j in range(NS):
        seen = seen | lax.shift_left(jnp.int32(1), block)
        after = plan[j % 2, block]
        closed = None
        if j % 2 == 1:
            closed = after == first
        walk.append((block, k, closed))
        if closed is None:
            block, k = after, k + 1
        else:
            free = ~seen & (seen + 1)
            lowest = jnp.int32(0)
            for i, bits in enumerate(BITS):
                lowest = lowest + jnp.where((free & bits) != 0, 1 << i, 0)
            first = jnp.where(closed, lowest, first)
            block = jnp.where(closed, lowest, after)
            k = jnp.where(closed, 0, k + 1)
    steps = []
    length = jnp.int32(0)
    for j in reversed(range(NS)):
        block, k, closed = walk[j]
        if closed is not None:
            length = jnp.where(closed, k + 1, length)
        m = lax.shift_right_logical(length, 1)
        out = k < m
        position = jnp.where(out, j + k, j - 3 * k + 2 * length - 1)
        onward = jnp.where(out, jnp.where(k == m - 1, 2, 0), jnp.where(k == length - 1, 2, 1))
        back = jnp.where(out, jnp.where(k == 0, 2, 1), jnp.where(k == m, 2, 0))
        steps.append((block, position, (onward, back) if j % 2 == 0 else (back, onward)))
    return steps


def tiles_kernel(scale, logder, block_of, plan, out, *scratch):
    (
        raw, blocks, pairs, place, table, sorted_rows, own, near, parts, pair_in, shares, y_in, halves, x_in,
        piece, mid, turned, home, local, send, rows_send, rows_recv, near_send, near_recv, pair_recv, y_recv, x_recv, chip_recv, mid_recv, home_recv,
    ) = scratch
    me = lax.axis_index("samp")
    par = lax.axis_index("par")
    z, x = me // 2, me % 2
    chip, core = par // 2, par % 2
    y, x_hi = chip // 2, chip % 2
    rows = raw.shape[0]
    per = rows // NS
    share = rows // (2 * CHIPS)
    units = len(parts)

    def ring(k):
        return jnp.where(k % 2 == 1, (k + 1) // 2, NS - k // 2)

    def along_y(d):
        return {"par": (lax.rem(y + d, NY) * 2 + x_hi) * 2 + core}

    def chip_at(offset):
        return lax.rem(y + offset[0], NY) * 2 + lax.rem(x_hi + offset[1], 2)

    def at_chip(to):
        return {"par": to * 2 + core}

    other_core = {"par": chip * 2 + 1 - core}
    other_x = {"par": (y * 2 + 1 - x_hi) * 2 + core}

    def remote(src, dst, send_sem, recv_sem, device):
        return pltpu.make_async_remote_copy(
            src_ref=src, dst_ref=dst, send_sem=send_sem, recv_sem=recv_sem, device_id=device, device_id_type=MESH
        )

    def await_bytes(ref, sem):
        pltpu.make_async_copy(ref, ref, sem).wait()

    arrivals = [
        pltpu.make_async_copy(plan, pairs, local.at[0]),
        pltpu.make_async_copy(block_of, blocks, local.at[1]),
        pltpu.make_async_copy(logder, raw, local.at[2]),
    ]
    for copy in arrivals:
        copy.start()

    barrier = pltpu.get_barrier_semaphore()

    def greet(k, carry):
        pl.semaphore_signal(barrier, inc=1, device_id={"samp": lax.rem(me + k, NS)}, device_id_type=MESH)
        return carry

    lax.fori_loop(1, NS, greet, 0)
    in_plane = [other_core] + [at_chip(chip_at(offset)) for offset in CHIP_OFFSETS]
    for device in in_plane:
        pl.semaphore_signal(barrier, inc=1, device_id=device, device_id_type=MESH)

    arrivals[0].wait()
    steps = ladder(pairs)
    arrivals[1].wait()
    block_at = lax.broadcasted_iota(jnp.int32, (NS, rows), 0)
    mine = block_at == blocks[...]
    earlier = lax.broadcasted_iota(jnp.int32, (rows, rows), 0) < lax.broadcasted_iota(jnp.int32, (rows, rows), 1)
    rank = jnp.dot(mine.astype(jnp.bfloat16), earlier.astype(jnp.bfloat16), preferred_element_type=jnp.float32)
    lane = lax.broadcasted_iota(jnp.int32, place.shape, 1)
    start = jnp.zeros((NS, rows), jnp.int32)
    placed = jnp.zeros(place.shape, jnp.int32)
    sides = [jnp.int32(0), jnp.int32(0)]
    for block, position, where in steps:
        start = jnp.where(block_at == block, position * per, start)
        placed = jnp.where(lane == block, position, placed)
        for r in range(2):
            sides[r] = jnp.where(position == me, where[r], sides[r])
    place[...] = placed
    to_table = pltpu.make_async_copy(place, table, local.at[3])
    to_table.start()
    spot = jnp.where(mine, rank.astype(jnp.int32) + start, 0)
    spot = jnp.sum(spot, axis=0, keepdims=True)
    pick = (lax.broadcasted_iota(jnp.int32, (rows, rows), 0) == spot).astype(jnp.bfloat16)
    arrivals[2].wait()
    sorted_rows[...] = jnp.dot(pick, raw[...], preferred_element_type=jnp.float32).astype(jnp.bfloat16)
    pl.semaphore_wait(barrier, NS - 1 + len(in_plane))

    def chunk(s):
        return pl.ds(pl.multiple_of(s * per, per), per)

    def send_rows(k, carry):
        to = lax.rem(me + ring(NS - k), NS)
        remote(sorted_rows.at[chunk(to)], own.at[chunk(me)], rows_send, rows_recv.at[NS - k], {"samp": to}).start()
        return carry

    lax.fori_loop(1, NS, send_rows, 0)
    own[chunk(me), :] = sorted_rows[chunk(me), :]
    to_table.wait()

    above = lax.rem(z + 1, NZ) * 2 + x
    below = lax.rem(z + NZ - 1, NZ) * 2 + x
    across = z * 2 + 1 - x
    def hand_on_chunk(s):
        for slot, to in ((1, above), (0, below), (2, across)):
            landing = near[0].at[slot, chunk(s)]
            remote(own.at[chunk(s)], landing, near_send.at[s // 2], near_recv.at[0, slot], {"samp": to}).start()

    @pl.when(me < 2 * EARLY)
    def _():
        hand_on_chunk(me)

    def arrive(k, carry):
        s = lax.rem(me + NS - ring(NS - k), NS)
        await_bytes(own.at[chunk(s)], rows_recv.at[NS - k])

        @pl.when(s < 2 * EARLY)
        def _():
            hand_on_chunk(s)

        return carry

    lax.fori_loop(1, NS, arrive, 0)

    step_rows = rows // STEPS
    handed = [EARLY]

    def hand_on(upto):
        for i in range(handed[0], upto):
            if i >= WINDOW:
                await_bytes(near[0].at[:, pl.ds(0, step_rows)], near_send.at[i - WINDOW])
            part = pl.ds(i * step_rows, step_rows)
            g = sum(i * step_rows >= first for first, _ in GROUPS) - 1
            there = pl.ds(i * step_rows - GROUPS[g][0], step_rows)
            for slot, to in ((1, above), (0, below), (2, across)):
                landing = near[g].at[slot, there]
                remote(own.at[part], landing, near_send.at[i], near_recv.at[g, slot], {"samp": to}).start()
        handed[0] = max(handed[0], upto)

    def multiply(other):
        return lax.dot_general(own[...], other, (((1,), (1,)), ((), ())), preferred_element_type=jnp.float32)

    def to_pair(u):
        remote(parts[u].at[1 - core], pair_in[u], send.at[u], pair_recv.at[u], other_core).start()

    def to_ys(u):
        await_bytes(pair_in[u], pair_recv.at[u])
        shares[u][...] = parts[u][core] + pair_in[u][...]
        if u in DIRECT:
            for i, offset in enumerate(CHIP_OFFSETS):
                to = chip_at(offset)
                remote(shares[u].at[to], y_in[u].at[i], send.at[units + u], chip_recv.at[u, i], at_chip(to)).start()
            return
        for d in (2, 1, 3):
            to = pl.ds(2 * lax.rem(y + d, NY), 2)
            remote(shares[u].at[to], y_in[u].at[d - 1], send.at[units + u], y_recv.at[u, d - 1], along_y(d)).start()

    def to_x(u):
        if u in DIRECT:
            return
        total = shares[u][pl.ds(2 * y, 2)]
        for i in range(NY - 1):
            await_bytes(y_in[u].at[i], y_recv.at[u, i])
            total += y_in[u][i]
        halves[u][...] = total
        remote(halves[u].at[1 - x_hi], x_in[u], send.at[2 * units + u], x_recv.at[u], other_x).start()

    def to_x(u):
        if u in DIRECT:
            return
        total = shares[u][pl.ds(2 * y, 2)]
        for i in range(NY - 1):
            await_bytes(y_in[u].at[i], y_recv.at[u, i])
            total += y_in[u][i]
        halves[u][...] = total
        remote(halves[u].at[1 - x_hi], x_in[u], send.at[2 * units + u], x_recv.at[u], other_x).start()

    def to_chips(u):
        await_bytes(pair_in[u], pair_recv.at[u])
        shares[u][...] = parts[u][core] + pair_in[u][...]
        for i, offset in enumerate(CHIP_OFFSETS):
            to = chip_at(offset)
            remote(shares[u].at[to], y_in[u].at[i], send.at[units + u], chip_recv.at[u, i], at_chip(to)).start()

    def whole(u):
        if u in DIRECT:
            total = shares[u][chip]
            for i in range(len(CHIP_OFFSETS)):
                await_bytes(y_in[u].at[i], chip_recv.at[u, i])
                total += y_in[u][i]
            return total * scale
        await_bytes(x_in[u], x_recv.at[u])
        return (halves[u][x_hi] + x_in[u][...]) * scale

    def own_tile(u):
        product = multiply(own[...])
        for c in range(2):
            for j in range(CHIPS):
                at = (2 * j + c) * share
                parts[u][c, j] = product[at : at + share]
        to_pair(u)

    def partner_tiles(u, g):
        for slot in range(3):
            await_bytes(near[g].at[slot], near_recv.at[g, slot])
        for r in range(2):
            product = multiply(near[g][sides[r]])
            for c in range(2):
                for j in range(CHIPS):
                    at = (2 * j + c) * share
                    parts[u][c, j, r] = product[at : at + share]
        to_pair(u)

    def exchange(src, landing, sem, recv_sem):
        def one(k, carry):
            to = lax.rem(me + ring(NS - k), NS)
            remote(src.at[to], landing.at[me], sem, recv_sem, {"samp": to}).start()
            return carry

        lax.fori_loop(1, NS, one, 0)
        landing[me] = src[me]

    def await_exchange(ref, sem):
        await_bytes(ref.at[pl.ds(0, NS - 1)], sem)

    sent_mid, sent_home = 3 * units, 3 * units + 3

    def to_mid(n):
        exchange(piece[n], mid[n], send.at[sent_mid + n], mid_recv.at[n])

    def to_home(n):
        await_exchange(mid[n], mid_recv.at[n])
        for b in range(NS):
            turned[n][b] = mid[n][table[0, b]]
        exchange(turned[n], home[n], send.at[sent_home + n], home_recv.at[n])

    def own_pieces():
        total = whole(0)
        for i in range(NS):
            a, l = 4 * (i // 4), 128 * (i % 4)
            piece[0][i] = total[a : a + 4, l : l + 128]

    def first_pieces():
        total = whole(1)
        for i in range(NS):
            r, a, l = i // 16, 4 * (i % 16 // 2), 128 * (i % 2)
            piece[1][i] = total[r, a : a + 4, l : l + 128]

    def later_pieces(h, total):
        for i in range(16):
            r, a = i // 8, 4 * (i % 8)
            piece[2][16 * h + i] = total[r, a : a + 4]

    hand_on(WINDOW)
    own_tile(0)
    hand_on(WINDOW + 2)
    to_ys(0)
    hand_on(12)
    to_x(0)
    hand_on(13)
    partner_tiles(1, 0)
    hand_on(14)
    to_ys(1)
    hand_on(STEPS)
    own_pieces()
    to_mid(0)
    partner_tiles(2, 1)
    to_ys(2)
    partner_tiles(3, 2)
    to_x(1)
    to_ys(3)
    to_x(2)
    to_home(0)
    first_pieces()
    to_mid(1)
    later_pieces(0, whole(2))
    later_pieces(1, whole(3))
    to_mid(2)
    await_exchange(home[0], home_recv.at[0])
    for i in range(NS):
        a, l = 4 * (i // 4), 128 * (i % 4)
        out[0, a : a + 4, l : l + 128] = home[0][i]
    to_home(1)
    to_home(2)
    await_exchange(home[1], home_recv.at[1])
    for i in range(NS):
        r, a, l = i // 16, 4 * (i % 16 // 2), 128 * (i % 2)
        out[1 + r, a : a + 4, l : l + 128] = home[1][i]
    await_exchange(home[2], home_recv.at[2])
    for i in range(NS):
        h, r, a = i // 16, i % 16 // 8, 4 * (i % 8)
        out[1 + r, a : a + 4, 256 + 128 * h : 384 + 128 * h] = home[2][i]

    await_bytes(own.at[pl.ds(0, rows - per)], rows_send)
    for i in range(STEPS - WINDOW, STEPS):
        await_bytes(near[0].at[:, pl.ds(0, step_rows)], near_send.at[i])
    for u in range(units):
        await_bytes(pair_in[u], send.at[u])
        await_bytes(y_in[u], send.at[units + u])
        if u not in DIRECT:
            await_bytes(x_in[u], send.at[2 * units + u])
    for n in range(3):
        await_exchange(piece[n], send.at[sent_mid + n])
        await_exchange(turned[n], send.at[sent_home + n])


def shards(logder, block_of, plan):
    rows, columns = logder.shape
    share = rows // (2 * CHIPS)
    hbm = pl.BlockSpec(memory_space=pltpu.HBM)
    scale = 1.0 / math.sqrt(columns * lax.axis_size("par"))
    f32, bf16, i32 = jnp.float32, jnp.bfloat16, jnp.int32
    kinds = ((share, rows),) + tuple((2, share, count) for _, count in GROUPS)
    sizes = (4, 4, 4)

    def buffers(*lead):
        return [pltpu.VMEM(lead + kind, f32) for kind in kinds]

    def pieces():
        return [pltpu.VMEM((NS, size, 128), f32) for size in sizes]

    sems = pltpu.SemaphoreType.DMA
    units = len(kinds)
    return pl.pallas_call(
        functools.partial(tiles_kernel, scale),
        name="tiles",
        out_shape=jax.ShapeDtypeStruct((3, share, rows), f32),
        in_specs=[hbm, hbm, hbm],
        out_specs=pl.BlockSpec(memory_space=pltpu.VMEM),
        scratch_shapes=[
            pltpu.VMEM((rows, columns), bf16),
            pltpu.VMEM((1, rows), i32),
            pltpu.SMEM((2, NS), i32),
            pltpu.VMEM((8, 128), i32),
            pltpu.SMEM((8, 128), i32),
            pltpu.VMEM((rows, columns), bf16),
            pltpu.VMEM((rows, columns), bf16),
            [pltpu.VMEM((3, count, columns), bf16) for _, count in GROUPS],
            buffers(2, CHIPS),
            buffers(CHIPS),
            buffers(CHIPS),
            [pltpu.VMEM(((CHIPS - 1,) if u in DIRECT else (NY - 1, 2)) + kind, f32) for u, kind in enumerate(kinds)],
            buffers(2),
            buffers(),
            pieces(),
            pieces(),
            pieces(),
            pieces(),
            sems((4,)),
            sems((3 * units + 2 * len(sizes),)),
            sems,
            sems((NS,)),
            sems((STEPS,)),
            sems((len(GROUPS), 3)),
            sems((units,)),
            sems((units, NY - 1)),
            sems((units,)),
            sems((units, CHIPS - 1)),
            sems((len(sizes),)),
            sems((len(sizes),)),
        ],
        compiler_params=pltpu.CompilerParams(
            collective_id=0, has_side_effects=True, vmem_limit_bytes=62 * 1024 * 1024
        ),
    )(logder, block_of.reshape(1, rows), plan)


def solution(mesh):
    return jax.shard_map(
        shards,
        mesh=mesh,
        in_specs=(P("samp", "par"), P("samp"), P()),
        out_specs=P(None, ("samp", "par"), None),
        check_vma=False,
    )
```
